512 devices in a mesh: dp: 2 (over x_hi), ffn: 16 (over z, core), hid: 16 (over y, x_lo).
Axes of the slice: x: 4 (x_hi: 2, x_lo: 2; x = x_hi * 2 + x_lo), y: 8, z: 8, core: 2. Of those that a mesh axis runs over, the one named last changes fastest.
Arguments:
- stream: bfloat16 [512, 16384], P('dp', 'hid'), may hold values from -160 to 160
- steering: float32 [16384], P('hid'), may hold values from -40 to 40
- strength: float32 [512], P('dp'), may hold values from 0.5 to 2
- norm_gain_vector: float32 [16384], P('hid'), may hold values from 0.25 to 1.75
- frozen_weights: bfloat16 [2, 16384, 26624], P('dp', 'hid', 'ffn'), may hold values from -0.046875 to 0.046875
- adapter_down_factors: bfloat16 [2, 16384, 16], P(None, 'hid'), may hold values from -0.046875 to 0.046875
- adapter_up_factors: bfloat16 [2, 16, 26624], P(None, None, 'ffn'), may hold values from -1.5 to 1.5
- cotangent: bfloat16 [512, 26624], P(('dp', 'hid'), 'ffn'), may hold values from -6 to 6
Outputs:
- residual_stream_gradient: bfloat16 [512, 16384], P('dp', 'hid')
- steering_vector_gradient: float32 [16384], P('hid')
- adapter_down_gradient: float32 [2, 16384, 16], P(None, 'hid')
- adapter_up_gradient: float32 [2, 16, 26624], P(None, None, 'ffn')
The draws below stay inside these ranges and needn't reach their ends.
All inputs are finite; a program needn't handle non-finite values.
Results may differ from the reference program's by a relative error of at most 0.0068.
Values may be sent and summed in bfloat16 or wider, within the bound.
A program may use at most 64 MiB of HBM per device.

```python
import math
import jax
import jax.numpy as jnp
from jax import lax

MODEL_WIDTH = 16384
HIDDEN_HALF = 26624
ADAPTER_RANK = 16
TOKENS = 512


def column_scales(key, count):
    ramp = jnp.exp(jnp.arange(count, dtype=jnp.float32) / count * math.log(3.0))
    spread = jnp.exp(jax.random.uniform(key, (count,), jnp.float32, 0.0, math.log(10.0))) / math.sqrt(10.0)
    return ramp * spread


def draw_stream(key, part):
    first, second, third = jax.random.split(jax.random.fold_in(key, 11), 3)
    columns = column_scales(second, MODEL_WIDTH)
    row_scale = jnp.exp(jax.random.uniform(third, (TOKENS, 1), jnp.float32, math.log(0.4), math.log(4.0)))
    base = jax.random.truncated_normal(first, -4.0, 4.0, (TOKENS, MODEL_WIDTH), jnp.float32)
    return (base * row_scale * columns[None, :]).astype(jnp.bfloat16)


def draw_steering(key, part):
    first, second = jax.random.split(jax.random.fold_in(key, 23), 2)
    columns = column_scales(second, MODEL_WIDTH)
    base = jax.random.truncated_normal(first, -4.0, 4.0, (MODEL_WIDTH,), jnp.float32)
    return base * columns


def levels(own_key, shape, cuts, smallest, high):
    level, own = 1.0, jax.random.fold_in(own_key, 6)
    for dim, parts in cuts:
        steps = jnp.exp(jax.random.uniform(jax.random.fold_in(own, dim), (parts,), jnp.float32, smallest / len(cuts), high / len(cuts)))
        level = level * jnp.repeat(steps, shape[dim] // parts).reshape([-1 if axis == dim else 1 for axis in range(len(shape))])
    return level


def gaussian(stream_key, shape, deviation, most, cuts=(), kind=jnp.bfloat16):
    array = deviation * jax.random.normal(stream_key, shape, jnp.float32)
    if cuts:
        array = array * levels(stream_key, shape, cuts, -0.22, 0.18)
    return jnp.clip(array, -most, most).astype(kind)


def setup_inputs(seed: int = 0) -> dict:
    key_of = jax.random.split(jax.random.key(seed), 9)
    stream = draw_stream(jax.random.fold_in(key_of[8], 71), 0)
    steering = draw_steering(jax.random.fold_in(key_of[8], 71), 0)
    strength = jnp.clip(jnp.exp(math.log(2.0) - 1.3862944 * jax.random.uniform(key_of[2], (TOKENS,), jnp.float32) ** levels(key_of[2], (TOKENS,), ((0, 2),), -0.2, 0.2)), 0.5, 2.0)
    norm_gain_vector = jnp.clip(1.0 + 0.15 * jax.random.normal(key_of[3], (MODEL_WIDTH,), jnp.float32), 0.25, 1.75)
    frozen_weights = gaussian(key_of[4], (2, MODEL_WIDTH, HIDDEN_HALF), MODEL_WIDTH ** -0.5, 0.046875, ((0, 2), (1, 16), (2, 16)))
    adapter_down_factors = gaussian(key_of[5], (2, MODEL_WIDTH, ADAPTER_RANK), MODEL_WIDTH ** -0.5, 0.046875, ((1, 16),))
    adapter_up_factors = gaussian(key_of[6], (2, ADAPTER_RANK, HIDDEN_HALF), ADAPTER_RANK ** -0.5, 1.5, ((2, 16),))
    cotangent = gaussian(key_of[7], (TOKENS, HIDDEN_HALF), 1.0, 6.0, ((0, 32), (1, 16)))
    return dict(stream=stream, steering=steering, strength=strength, norm_gain_vector=norm_gain_vector, frozen_weights=frozen_weights, adapter_down_factors=adapter_down_factors, adapter_up_factors=adapter_up_factors, cotangent=cotangent)


ADAPTER_SCALE = 0.5

def reference(stream, steering, strength, norm_gain_vector, frozen_weights, adapter_down_factors, adapter_up_factors, cotangent):
    rows = stream.astype(jnp.float32)
    stream_ms = lax.optimization_barrier(jnp.mean(rows * rows, axis=1)) + 1e-06
    steer_ms = jnp.mean(steering * steering) + 1e-06
    scale = strength * jnp.sqrt(stream_ms / steer_ms)
    steered = rows + scale[:, None] * steering[None, :]
    inv_rms = lax.rsqrt(lax.optimization_barrier(jnp.mean(steered * steered, axis=1)) + 1e-05)
    normalized_input = (steered * inv_rms[:, None] * norm_gain_vector[None, :]).astype(jnp.bfloat16)
    lowrank_rows = jnp.einsum('jq,hqp->jhp', normalized_input.astype(jnp.float32), adapter_down_factors.astype(jnp.float32)).astype(jnp.bfloat16)
    gate_values = jnp.dot(normalized_input, frozen_weights[0], preferred_element_type=jnp.float32)
    gate_values = gate_values + ADAPTER_SCALE * jnp.dot(lowrank_rows[:, 0].astype(jnp.float32), adapter_up_factors[0].astype(jnp.float32))
    up_projection_values = jnp.dot(normalized_input, frozen_weights[1], preferred_element_type=jnp.float32)
    up_projection_values = up_projection_values + ADAPTER_SCALE * jnp.dot(lowrank_rows[:, 1].astype(jnp.float32), adapter_up_factors[1].astype(jnp.float32))
    sigma = jax.nn.sigmoid(gate_values)
    incoming_gradient = cotangent.astype(jnp.float32)
    gate_grad = incoming_gradient * up_projection_values * sigma * (1.0 + gate_values * (1.0 - sigma))
    upper_grad = incoming_gradient * gate_values * sigma
    activation_gradient = jnp.stack([gate_grad, upper_grad], axis=1).astype(jnp.bfloat16)
    lowrank_backward = jnp.einsum('sua,uqa->suq', activation_gradient.astype(jnp.float32), adapter_up_factors.astype(jnp.float32)).astype(jnp.bfloat16)
    normalized_gradient = jnp.dot(activation_gradient[:, 0], frozen_weights[0].T, preferred_element_type=jnp.float32)
    normalized_gradient = normalized_gradient + jnp.dot(activation_gradient[:, 1], frozen_weights[1].T, preferred_element_type=jnp.float32)
    normalized_gradient = normalized_gradient + ADAPTER_SCALE * jnp.einsum('qme,mfe->qf', lowrank_backward.astype(jnp.float32), adapter_down_factors.astype(jnp.float32))
    product = lax.optimization_barrier(jnp.mean(steered * norm_gain_vector[None, :] * normalized_gradient, axis=1))
    steered_grad = inv_rms[:, None] * norm_gain_vector[None, :] * normalized_gradient - (inv_rms ** 3 * product)[:, None] * steered
    residual_stream_gradient = steered_grad.astype(jnp.bfloat16)
    steering_vector_gradient = lax.optimization_barrier(jnp.sum(scale[:, None] * steered_grad, axis=0))
    adapter_down_gradient = ADAPTER_SCALE * jnp.einsum('cl,can->aln', normalized_input.astype(jnp.float32), lowrank_backward.astype(jnp.float32))
    adapter_up_gradient = ADAPTER_SCALE * jnp.einsum('qyj,qyi->yji', lowrank_rows.astype(jnp.float32), activation_gradient.astype(jnp.float32))
    return (residual_stream_gradient, steering_vector_gradient, adapter_down_gradient, adapter_up_gradient)
```

```python
import functools

import jax
import jax.numpy as jnp
from jax import lax
from jax.experimental import pallas as pl
from jax.experimental.pallas import tpu as pltpu
from jax.sharding import PartitionSpec as P

ADAPTER_SCALE = 0.5
RANK = 16
ROWS = 16
LANES = 128
MESH = pl.DeviceIdType.MESH
F32 = jnp.float32
BF16 = jnp.bfloat16
NT = (((1,), (1,)), ((), ()))
N_SEMS = 160


def tiles(total, size):
    return [(at, min(size, total - at)) for at in range(0, total, size)]


def row_to_columns(row):
    return jnp.transpose(jnp.broadcast_to(row, (LANES, row.shape[1])))


def columns_to_row(partial):
    return jnp.sum(jnp.transpose(partial), axis=0, keepdims=True)


def kernel(
    model_width, n_hid, n_ffn,
    x_ref, steer_ref, strength_ref, gain_ref, w_hbm, down_ref, up_ref, cot_ref,
    out_ref, steer_grad_ref, down_grad_ref, up_grad_ref,
    w_buf, x_other, stat_a, stat_b, stat_mine, stat_other, steered, cols, normed, partial, y_send, y_recv,
    y_sum, y_block, x_recv, up_ext, down_ext, acts_all, acts_other, back, core_recv, core_sum,
    z_send, z_recv, z_sum, dp_main, dp_ext, gathered, up_mine, up_theirs, steer_mine, steer_theirs,
    send_sem, recv_sem, local_sem,
):
    tokens, width = x_ref.shape
    hidden = w_hbm.shape[1]
    n_y, n_z = n_hid // 2, n_ffn // 2
    dp, fi, hi = lax.axis_index("dp"), lax.axis_index("ffn"), lax.axis_index("hid")
    y, xl, z, core = hi // 2, hi % 2, fi // 2, fi % 2
    first = dp == 0

    to_dp = {"dp": 1 - dp}
    to_xl = {"hid": hi + 1 - 2 * xl}
    to_diag = {"dp": 1 - dp, "hid": hi + 1 - 2 * xl}
    to_core = {"ffn": fi + 1 - 2 * core}
    y_next = ({"hid": lax.rem(hi + 2, n_hid)}, {"hid": lax.rem(hi + n_hid - 2, n_hid)})
    z_next = ({"ffn": lax.rem(fi + 2, n_ffn)}, {"ffn": lax.rem(fi + n_ffn - 2, n_ffn)})

    w_copy = pltpu.make_async_copy(w_hbm, w_buf, local_sem)
    w_copy.start()

    peers = [{"hid": lax.rem(hi + i, n_hid)} for i in range(1, n_hid)]
    peers += [to_dp, to_diag, to_core, *z_next]
    barrier = pltpu.get_barrier_semaphore()
    for peer in peers:
        pl.semaphore_signal(barrier, inc=1, device_id=peer, device_id_type=MESH)
    pl.semaphore_wait(barrier, len(peers))

    started = []

    def send(src, dst, device):
        i = len(started)
        copy = pltpu.make_async_remote_copy(
            src_ref=src, dst_ref=dst, send_sem=send_sem.at[i], recv_sem=recv_sem.at[i],
            device_id=device, device_id_type=MESH,
        )
        copy.start()
        started.append(copy)
        return copy

    half = tokens // 2
    mine = pl.ds(pl.multiple_of(core * half, half), half)
    stream_in = send(x_ref.at[mine], x_other.at[mine], to_dp)

    def sum_over_hid(slots, value):
        slots[hi] = value
        copies = [
            send(slots.at[hi], slots.at[hi], {"hid": lax.rem(hi + i, n_hid)}) for i in range(1, n_hid)
        ]
        for copy in copies:
            copy.wait_recv()
        total = slots[0]
        for i in range(1, n_hid):
            total = total + slots[i]
        return total

    lanes = tiles(width, LANES)
    steer = steer_ref[...]
    gain = gain_ref[...]

    squares = jnp.zeros((tokens, LANES), F32)
    for at, size in lanes:
        piece = x_ref[:, at:at + size].astype(F32)
        squares += piece * piece
    steer_power = jnp.sum(steer * steer, axis=1, keepdims=True)
    sub = lax.broadcasted_iota(jnp.int32, (8, tokens), 0)
    powers = sum_over_hid(
        stat_a,
        jnp.where(
            sub == 0,
            jnp.broadcast_to(columns_to_row(squares), (8, tokens)),
            jnp.broadcast_to(steer_power, (8, tokens)),
        ),
    )
    stream_ms = powers[0:1] / model_width + 1e-06
    steer_ms = powers[1:2] / model_width + 1e-06
    scale = strength_ref[...] * jnp.sqrt(stream_ms / steer_ms)

    scale_cols = row_to_columns(scale)
    cols[0] = scale_cols
    squares = jnp.zeros((tokens, LANES), F32)
    for at, size in lanes:
        piece = x_ref[:, at:at + size].astype(F32) + scale_cols * steer[:, at:at + size]
        steered[:, at:at + size] = piece
        squares += piece * piece
    power = sum_over_hid(stat_b, jnp.broadcast_to(columns_to_row(squares), (8, tokens)))
    inv = lax.rsqrt(power[0:1] / model_width + 1e-05)
    stat_mine[...] = jnp.where(
        sub == 0, jnp.broadcast_to(scale, (8, tokens)), jnp.broadcast_to(inv, (8, tokens))
    )
    stat_in = send(stat_mine, stat_other, to_dp)
    inv_cols = row_to_columns(inv)
    cols[1] = inv_cols
    for at, size in lanes:
        normed[0, :, at:at + size] = (
            steered[:, at:at + size] * inv_cols * gain[:, at:at + size]
        ).astype(BF16)

    up_ext[...] = jnp.zeros(up_ext.shape, BF16)
    up_ext[0:2 * RANK, 0:hidden] = up_ref[...]
    row = lax.broadcasted_iota(jnp.int32, (LANES, LANES), 0)
    col = lax.broadcasted_iota(jnp.int32, (LANES, LANES), 1)
    up_ext[:, hidden:] = jnp.where((row == 32) & ((col == 32) | (col == 33)), 1.0, 0.0).astype(BF16)
    down_ext[...] = jnp.zeros(down_ext.shape, BF16)
    down_ext[0:2 * RANK, :] = down_ref[...]

    w_copy.wait()

    def forward(which):
        rows = normed[which]
        for at, size in tiles(hidden, 256):
            block = jnp.dot(rows, w_buf[:, at:at + size], preferred_element_type=F32)
            partial[which, :, :, at:at + size] = block.reshape(n_y, 2 * ROWS, size)
        block = lax.dot_general(rows, down_ext[...], NT, preferred_element_type=F32)
        partial[which, :, :, hidden:] = block.reshape(n_y, 2 * ROWS, LANES)

    def hops(n, s, d):
        return n // 2 if (s + d) % 2 == 0 else n // 2 - 1

    def reduce_step(n, me, terms, sends, recvs, nexts, flying, s, d, j):
        count = hops(n, s, d)
        if j >= count:
            return
        k = count - j
        owner = lax.rem(me + (k if d == 0 else n - k), n)
        value = terms[s, owner]
        if j:
            flying[s, d, j - 1].wait_recv()
            value = value + recvs[s, d, j - 1].astype(F32)
        sends[s, d, j] = value.astype(BF16)
        flying[s, d, j] = send(sends.at[s, d, j], recvs.at[s, d, j], nexts[d])

    def reduce_end(n, me, terms, recvs, flying, s):
        value = terms[s, me]
        for d in (0, 1):
            count = hops(n, s, d)
            if count:
                flying[s, d, count - 1].wait_recv()
                value = value + recvs[s, d, count - 1].astype(F32)
        return value

    def gather_step(n, me, held, nexts, flying, s, d, j):
        if j >= hops(n, s, d):
            return
        if j:
            flying[s, d, j - 1].wait_recv()
        origin = lax.rem(me + (n - j if d == 0 else j), n)
        flying[s, d, j] = send(held.at[s, origin], held.at[s, origin], nexts[d])

    y_args = (n_y, y, partial, y_send, y_recv, y_next, {})
    forward(0)
    for d in (0, 1):
        reduce_step(*y_args, 0, d, 0)

    stream_in.wait_recv()
    stream_core = send(x_other.at[mine], x_other.at[mine], to_core)
    stat_in.wait_recv()
    stream_core.wait_recv()
    scale_other = row_to_columns(stat_other[0:1])
    inv_other = row_to_columns(stat_other[1:2])
    for at, size in lanes:
        piece = x_other[:, at:at + size].astype(F32) + scale_other * steer[:, at:at + size]
        normed[1, :, at:at + size] = (piece * inv_other * gain[:, at:at + size]).astype(BF16)
    forward(1)
    for d in (0, 1):
        reduce_step(*y_args, 1, d, 0)
    for j in range(1, n_y // 2):
        for s in (0, 1):
            for d in (0, 1):
                reduce_step(*y_args, s, d, j)
    x_in = []
    for s in (0, 1):
        total = reduce_end(n_y, y, partial, y_recv, y_args[-1], s).reshape(2, ROWS, hidden + LANES)
        y_sum[s] = total
        y_block[s] = total.astype(BF16)
        if s == 0:
            x_in.append(send(y_block.at[0, 1 - xl], x_recv.at[0], to_xl))
        else:
            x_in.append(send(y_block.at[1, xl], x_recv.at[1], to_dp))
            x_in.append(send(y_block.at[1, 1 - xl], x_recv.at[2], to_diag))
    for copy in x_in:
        copy.wait_recv()

    acts_same = y_sum[0, xl] + x_recv[0].astype(F32)
    acts_cross = x_recv[1].astype(F32) + x_recv[2].astype(F32)
    gate = jnp.where(first, acts_same, acts_cross)
    up = jnp.where(first, acts_cross, acts_same)
    lane = lax.broadcasted_iota(jnp.int32, (ROWS, LANES), 1)
    low_gate = jnp.where(lane < RANK, gate[:, hidden:], 0.0).astype(BF16)
    low_up = jnp.where((lane >= RANK) & (lane < 2 * RANK), up[:, hidden:], 0.0).astype(BF16)
    factors = up_ext[:, 0:hidden]
    gate = gate[:, 0:hidden] + ADAPTER_SCALE * jnp.dot(low_gate, factors, preferred_element_type=F32)
    up = up[:, 0:hidden] + ADAPTER_SCALE * jnp.dot(low_up, factors, preferred_element_type=F32)
    sigma = 1.0 / (1.0 + jnp.exp(-gate))
    flow = cot_ref[...].astype(F32)
    gate_grad = (flow * up * sigma * (1.0 + gate * (1.0 - sigma))).astype(BF16)
    upper_grad = (flow * gate * sigma).astype(BF16)

    def ext_columns(low, grad, acts):
        inner = jnp.sum(grad.astype(F32) * acts, axis=1, keepdims=True)
        high = inner.astype(BF16).astype(F32)
        rest = jnp.where(lane == 32, high, jnp.where(lane == 33, inner - high, 0.0))
        return low.astype(F32) + rest

    gate_ext = ext_columns(low_gate, gate_grad, gate)
    upper_ext = ext_columns(low_up, upper_grad, up)
    gate_grad, upper_grad = gate_grad.astype(F32), upper_grad.astype(F32)
    acts_all[0, y, xl, :, 0:hidden] = jnp.where(first, gate_grad, upper_grad).astype(BF16)
    acts_all[0, y, xl, :, hidden:] = jnp.where(first, gate_ext, upper_ext).astype(BF16)
    acts_other[:, 0:hidden] = jnp.where(first, upper_grad, gate_grad).astype(BF16)
    acts_other[:, hidden:] = jnp.where(first, upper_ext, gate_ext).astype(BF16)

    x_out = [
        send(acts_all.at[0, y, xl], acts_all.at[0, y, xl], to_xl),
        send(acts_other, acts_all.at[1, y, xl], to_dp),
        send(acts_other, acts_all.at[1, y, xl], to_diag),
    ]
    g_args = (n_y, y, acts_all, y_next, {})
    x_out[0].wait_recv()
    for d in (0, 1):
        gather_step(*g_args, 0, d, 0)
    x_out[1].wait_recv()
    x_out[2].wait_recv()
    for d in (0, 1):
        gather_step(*g_args, 1, d, 0)
    for j in range(1, n_y // 2):
        for s in (0, 1):
            for d in (0, 1):
                gather_step(*g_args, s, d, j)

    wide = lax.broadcasted_iota(jnp.int32, (tokens, LANES), 1)
    keep = ((wide >= RANK * dp) & (wide < RANK * dp + RANK)) | (wide == 32)

    def backward(which):
        for at, size in tiles(width, 256):
            rows = acts_all[which, :, :, :, 0:hidden].reshape(tokens, hidden)
            block = lax.dot_general(rows, w_buf[at:at + size, :], NT, preferred_element_type=F32)
            back[which, :, :, :, at:at + size] = block.reshape(n_z, 2, ROWS, size)
        rows = acts_all[which].reshape(tokens, hidden + LANES)
        block = lax.dot_general(rows, up_ext[...], NT, preferred_element_type=F32)
        back[which, :, :, :, width:] = jnp.where(keep, block, 0.0).reshape(n_z, 2, ROWS, LANES)

    core_in = []
    for s in (0, 1):
        for d in (0, 1):
            count = hops(n_y, s, d)
            if count:
                g_args[-1][s, d, count - 1].wait_recv()
        backward(s)
        core_in.append(send(back.at[s, :, 1 - core], core_recv.at[s], to_core))

    total = jnp.zeros((RANK, hidden), F32)
    for s in (0, 1):
        low = acts_all[s, :, :, :, hidden:].reshape(tokens, LANES).astype(F32)
        low = jnp.transpose(low)
        low = jnp.where(first, low[0:RANK], low[RANK:2 * RANK]).astype(BF16)
        rows = acts_all[s, :, :, :, 0:hidden].reshape(tokens, hidden)
        total += jnp.dot(low, rows, preferred_element_type=F32)
    up_mine[...] = ADAPTER_SCALE * total
    up_in = send(up_mine, up_theirs, to_dp)

    z_args = (n_z, z, core_sum, z_send, z_recv, z_next, {})
    for s in (0, 1):
        core_in[s].wait_recv()
        core_sum[s] = back[s, :, core] + core_recv[s]
        for d in (0, 1):
            reduce_step(*z_args, s, d, 0)
    for j in range(1, n_z // 2):
        for s in (0, 1):
            for d in (0, 1):
                reduce_step(*z_args, s, d, j)
    z_sum[1] = reduce_end(n_z, z, core_sum, z_recv, z_args[-1], 1)
    main_in = send(z_sum.at[1], dp_main, to_dp)
    z_sum[0] = reduce_end(n_z, z, core_sum, z_recv, z_args[-1], 0)
    dp_mine = z_sum.at[0, :, width:]
    ext_in = send(dp_mine, dp_ext, to_dp)
    main_in.wait_recv()
    ext_in.wait_recv()

    share = pl.ds(pl.multiple_of(fi * ROWS, ROWS), ROWS)
    own_ext = z_sum[0, :, width:] + dp_main[:, width:]
    low_own = own_ext.astype(BF16)
    low_other = (z_sum[1, :, width:] + dp_ext[...]).astype(BF16)
    normed_grad = (
        z_sum[0, :, 0:width]
        + dp_main[:, 0:width]
        + ADAPTER_SCALE * jnp.dot(low_own, down_ext[...], preferred_element_type=F32)
    )
    inv_here = cols[1, share]
    inner = jnp.sum(jnp.where(lane == 32, own_ext, 0.0), axis=1, keepdims=True) / model_width
    pull = inv_here * inv_here * inner
    for at, size in lanes:
        gathered[0, z, core, :, at:at + size] = (
            inv_here * gain[:, at:at + size] * normed_grad[:, at:at + size]
            - pull * steered[share, at:at + size]
        ).astype(BF16)
    gathered[0, z, core, :, width:width + LANES] = low_own
    gathered[0, z, core, :, width + LANES:] = low_other

    flying = {}
    mine_core = []
    held = gathered.at[0]

    def spread(origin):
        mine_core.append(send(held.at[origin, core], held.at[origin, core], to_core))

    spread(z)
    for j in range(n_z // 2):
        for d in (0, 1):
            count = hops(n_z, 0, d)
            if j < count:
                origin = lax.rem(z + (n_z - j if d == 0 else j), n_z)
                flying[d, j] = send(held.at[origin, core], held.at[origin, core], z_next[d])
        for d in (0, 1):
            count = hops(n_z, 0, d)
            if j < count:
                flying[d, j].wait_recv()
                spread(lax.rem(z + (n_z - j - 1 if d == 0 else j + 1), n_z))
    for copy in mine_core:
        copy.wait_recv()

    for at, size in lanes:
        piece = gathered[0, :, :, :, at:at + size].reshape(tokens, size)
        out_ref[:, at:at + size] = piece
        steer_mine[:, at:at + size] = jnp.sum(cols[0] * piece.astype(F32), axis=0, keepdims=True)
    steer_in = send(steer_mine, steer_theirs, to_dp)
    down = []
    for s in (0, 1):
        low = gathered[0, :, :, :, width + s * LANES:width + (s + 1) * LANES]
        low = jnp.transpose(low.reshape(tokens, LANES).astype(F32))[0:2 * RANK].astype(BF16)
        down.append(jnp.dot(low, normed[s], preferred_element_type=F32))
    down_grad_ref[...] = ADAPTER_SCALE * (down[0] + down[1])
    up_in.wait_recv()
    up_grad_ref[dp] = up_mine[...]
    up_grad_ref[1 - dp] = up_theirs[...]
    steer_in.wait_recv()
    steer_grad_ref[...] = steer_mine[...] + steer_theirs[...]
    for copy in started:
        copy.wait_send()


def solution(mesh):
    n_hid, n_ffn = mesh.shape["hid"], mesh.shape["ffn"]
    n_y, n_z = n_hid // 2, n_ffn // 2

    def local(stream, steering, strength, gain, weights, down, up, cotangent):
        tokens, width = stream.shape
        hidden = weights.shape[2]
        vmem = pl.BlockSpec(memory_space=pltpu.VMEM)
        ext = hidden + LANES
        y_hop = (2, 2, n_y // 2, 2 * ROWS, ext)
        z_hop = (2, 2, n_z // 2, ROWS, width + LANES)
        scratch = [
            ((width, hidden), BF16),
            ((tokens, width), BF16),
            ((n_hid, 8, tokens), F32),
            ((n_hid, 8, tokens), F32),
            ((8, tokens), F32),
            ((8, tokens), F32),
            ((tokens, width), F32),
            ((2, tokens, LANES), F32),
            ((2, tokens, width), BF16),
            ((2, n_y, 2 * ROWS, ext), F32),
            (y_hop, BF16),
            (y_hop, BF16),
            ((2, 2, ROWS, ext), F32),
            ((2, 2, ROWS, ext), BF16),
            ((3, ROWS, ext), BF16),
            ((LANES, ext), BF16),
            ((LANES, width), BF16),
            ((2, n_y, 2, ROWS, ext), BF16),
            ((ROWS, ext), BF16),
            ((2, n_z, 2, ROWS, width + LANES), F32),
            ((2, n_z, ROWS, width + LANES), F32),
            ((2, n_z, ROWS, width + LANES), F32),
            (z_hop, BF16),
            (z_hop, BF16),
            ((2, ROWS, width + LANES), F32),
            ((ROWS, width + LANES), F32),
            ((ROWS, LANES), F32),
            ((1, n_z, 2, ROWS, width + 2 * LANES), BF16),
            ((RANK, hidden), F32),
            ((RANK, hidden), F32),
            ((1, width), F32),
            ((1, width), F32),
        ]
        model_width = width * n_hid
        residual, steer_grad, down_grad, up_grad = pl.pallas_call(
            functools.partial(kernel, model_width, n_hid, n_ffn),
            out_shape=(
                jax.ShapeDtypeStruct((tokens, width), BF16),
                jax.ShapeDtypeStruct((1, width), F32),
                jax.ShapeDtypeStruct((2 * RANK, width), F32),
                jax.ShapeDtypeStruct((2, RANK, hidden), F32),
            ),
            in_specs=[vmem] * 4 + [pl.BlockSpec(memory_space=pl.ANY)] + [vmem] * 3,
            out_specs=(vmem,) * 4,
            scratch_shapes=[pltpu.VMEM(shape, dtype) for shape, dtype in scratch]
            + [
                pltpu.SemaphoreType.DMA((N_SEMS,)),
                pltpu.SemaphoreType.DMA((N_SEMS,)),
                pltpu.SemaphoreType.DMA,
            ],
            compiler_params=pltpu.CompilerParams(
                collective_id=0, has_side_effects=True, vmem_limit_bytes=60 * 1024 * 1024
            ),
            cost_estimate=pl.CostEstimate(
                flops=8 * tokens * width * hidden, bytes_accessed=2 * width * hidden, transcendentals=0
            ),
        )(
            stream,
            steering.reshape(1, width),
            strength.reshape(1, tokens),
            gain.reshape(1, width),
            weights.reshape(width, hidden),
            jnp.transpose(down, (0, 2, 1)).reshape(2 * RANK, width),
            up.reshape(2 * RANK, hidden),
            cotangent,
        )
        return (
            residual,
            steer_grad.reshape(width),
            jnp.transpose(down_grad.reshape(2, RANK, width), (0, 2, 1)),
            up_grad,
        )

    in_specs = (
        P("dp", "hid"),
        P("hid"),
        P("dp"),
        P("hid"),
        P("dp", "hid", "ffn"),
        P(None, "hid", None),
        P(None, None, "ffn"),
        P(("dp", "hid"), "ffn"),
    )
    out_specs = (P("dp", "hid"), P("hid"), P(None, "hid", None), P(None, None, "ffn"))
    return jax.shard_map(local, mesh=mesh, in_specs=in_specs, out_specs=out_specs, check_vma=False)
```

```python
import functools

import jax
import jax.numpy as jnp
from jax import lax
from jax.experimental import pallas as pl
from jax.experimental.pallas import tpu as pltpu
from jax.sharding import PartitionSpec as P

ADAPTER_SCALE = 0.5
RANK = 16
ROWS = 16
LANES = 128
MESH = pl.DeviceIdType.MESH
F32 = jnp.float32
BF16 = jnp.bfloat16
NT = (((1,), (1,)), ((), ()))
N_SEMS = 192


def tiles(total, size):
    return [(at, min(size, total - at)) for at in range(0, total, size)]


def row_to_columns(row):
    return jnp.transpose(jnp.broadcast_to(row, (LANES, row.shape[1])))


def columns_to_row(partial):
    return jnp.sum(jnp.transpose(partial), axis=0, keepdims=True)


def kernel(
    model_width, n_hid, n_ffn,
    x_ref, steer_ref, strength_ref, gain_ref, w_hbm, down_ref, up_ref, cot_ref,
    out_ref, steer_grad_ref, down_grad_ref, up_grad_ref,
    w_buf, x_other, stat_a, stat_b, ratio_mine, ratio_theirs, steered, cols, normed, partial, y_send, y_recv,
    y_block, x_recv, up_ext, down_ext, acts_all, acts_other, back, core_recv,
    z_send, z_recv, own_sum, gathered, low_mine, low_theirs, up_mine, up_theirs, steer_mine, steer_theirs,
    send_sem, recv_sem, z_send_sem, z_recv_sem, g_send_sem, g_recv_sem, local_sem,
):
    tokens, width = x_ref.shape
    hidden = w_hbm.shape[1]
    n_y, n_z = n_hid // 2, n_ffn // 2
    dp, fi, hi = lax.axis_index("dp"), lax.axis_index("ffn"), lax.axis_index("hid")
    y, xl, z, core = hi // 2, hi % 2, fi // 2, fi % 2
    first = dp == 0

    to_dp = {"dp": 1 - dp}
    to_xl = {"hid": hi + 1 - 2 * xl}
    to_diag = {"dp": 1 - dp, "hid": hi + 1 - 2 * xl}
    to_core = {"ffn": fi + 1 - 2 * core}
    y_next = ({"hid": lax.rem(hi + 2, n_hid)}, {"hid": lax.rem(hi + n_hid - 2, n_hid)})

    w_copy = pltpu.make_async_copy(w_hbm, w_buf, local_sem)
    w_copy.start()

    peers = [{"hid": lax.rem(hi + i, n_hid)} for i in range(1, n_hid)]
    peers += [{"dp": 1 - dp, "hid": lax.rem(hi + i, n_hid)} for i in range(n_hid)]
    for i in range(1, n_z):
        peers += [{"ffn": lax.rem(z + i, n_z) * 2 + core}]
        peers += [{"dp": 1 - dp, "ffn": lax.rem(z + i, n_z) * 2 + core}]
    peers += [to_core]
    barrier = pltpu.get_barrier_semaphore()
    for peer in peers:
        pl.semaphore_signal(barrier, inc=1, device_id=peer, device_id_type=MESH)
    pl.semaphore_wait(barrier, len(peers))

    started = []

    def send(src, dst, device):
        i = len(started)
        copy = pltpu.make_async_remote_copy(
            src_ref=src, dst_ref=dst, send_sem=send_sem.at[i], recv_sem=recv_sem.at[i],
            device_id=device, device_id_type=MESH,
        )
        copy.start()
        started.append(copy)
        return copy

    half = tokens // 2
    mine = pl.ds(pl.multiple_of(core * half, half), half)

    lanes = tiles(width, LANES)
    steer = steer_ref[...]
    gain = gain_ref[...]
    sub = lax.broadcasted_iota(jnp.int32, (4, tokens), 0)

    def share_stats(slots, value, batches):
        slots[0, hi] = value
        copies = []
        for i in range(n_hid):
            there = {"dp": 1 - dp, "hid": lax.rem(hi + i, n_hid)}
            if i:
                copies.append(send(slots.at[0, hi], slots.at[0, hi], {"hid": lax.rem(hi + i, n_hid)}))
            if batches == 2:
                copies.append(send(slots.at[0, hi], slots.at[1, hi], there))
        return copies

    def total_stats(slots, which):
        total = slots[which, 0]
        for i in range(1, n_hid):
            total = total + slots[which, i]
        return total

    squares = jnp.zeros((tokens, LANES), F32)
    crosses = jnp.zeros((tokens, LANES), F32)
    for at, size in lanes:
        piece = x_ref[:, at:at + size].astype(F32)
        squares += piece * piece
        crosses += piece * steer[:, at:at + size]
    steer_power = jnp.sum(steer * steer, axis=1, keepdims=True)
    rows = (columns_to_row(squares), steer_power, columns_to_row(crosses), strength_ref[...])
    packed = jnp.broadcast_to(rows[0], (4, tokens))
    for i in (1, 2, 3):
        packed = jnp.where(sub == i, jnp.broadcast_to(rows[i], (4, tokens)), packed)
    stat_in = share_stats(stat_a, packed, 2)
    stream_in = send(x_ref.at[mine], x_other.at[mine], to_dp)
    for copy in stat_in:
        copy.wait_recv()

    def rescale(which):
        total = total_stats(stat_a, which)
        power, steer_total, cross = total[0:1], total[1:2], total[2:3]
        scale = stat_a[which, 0, 3:4] * jnp.sqrt(
            (power / model_width + 1e-06) / (steer_total / model_width + 1e-06)
        )
        steered_power = power + scale * (2.0 * cross + scale * steer_total)
        steered_power = jnp.maximum(steered_power, 1e-07 * power)
        return scale, lax.rsqrt(steered_power / model_width + 1e-05)

    scale, inv_first = rescale(0)
    scale_other, inv_first_other = rescale(1)
    scale_cols = row_to_columns(scale)
    inv_cols = row_to_columns(inv_first)
    cols[0] = scale_cols
    squares = jnp.zeros((tokens, LANES), F32)
    for at, size in lanes:
        piece = x_ref[:, at:at + size].astype(F32) + scale_cols * steer[:, at:at + size]
        steered[:, at:at + size] = piece
        squares += piece * piece
        normed[0, :, at:at + size] = (piece * inv_cols * gain[:, at:at + size]).astype(BF16)

    up_ext[...] = jnp.zeros(up_ext.shape, BF16)
    up_ext[0:2 * RANK, 0:hidden] = up_ref[...]
    row = lax.broadcasted_iota(jnp.int32, (LANES, LANES), 0)
    col = lax.broadcasted_iota(jnp.int32, (LANES, LANES), 1)
    up_ext[:, hidden:] = jnp.where((row == 32) & ((col == 32) | (col == 33)), 1.0, 0.0).astype(BF16)
    down_ext[...] = jnp.zeros(down_ext.shape, BF16)
    down_ext[0:2 * RANK, :] = down_ref[...]

    w_copy.wait()

    def forward(which):
        rows = normed[which]
        for at, size in tiles(hidden, 256):
            block = jnp.dot(rows, w_buf[:, at:at + size], preferred_element_type=F32)
            partial[which, :, :, :, at:at + size] = block.reshape(n_y, 2, ROWS, size)
        block = lax.dot_general(rows, down_ext[...], NT, preferred_element_type=F32)
        partial[which, :, :, :, hidden:] = block.reshape(n_y, 2, ROWS, LANES)

    def hops(n, b, d):
        return n // 2 if (b + d) % 2 == 0 else n // 2 - 1

    sums_of = ((0, 1 - xl), (1, xl), (1, 1 - xl), (0, xl))

    def reduce_step(n, me, terms, sends, recvs, nexts, flying, b, d, j):
        count = hops(n, b, d)
        if j >= count:
            return
        k = count - j
        owner = lax.rem(me + (k if d == 0 else n - k), n)
        batch, low = sums_of[b]
        value = terms[batch, owner, low]
        if j:
            flying[b, d, j - 1].wait_recv()
            value = value + recvs[b, d, j - 1].astype(F32)
        sends[b, d, j] = value.astype(BF16)
        flying[b, d, j] = send(sends.at[b, d, j], recvs.at[b, d, j], nexts[d])

    def reduce_end(n, me, terms, sends, recvs, nexts, flying, b):
        batch, low = sums_of[b]
        value = terms[batch, me, low]
        for d in (0, 1):
            count = hops(n, b, d)
            if count:
                flying[b, d, count - 1].wait_recv()
                value = value + recvs[b, d, count - 1].astype(F32)
        return value

    grads_of = ((0, xl), (0, 1 - xl), (1, xl), (1, 1 - xl))

    def gather_step(n, me, held, nexts, flying, b, d, j):
        if j >= hops(n, b, d):
            return
        if j:
            flying[b, d, j - 1].wait_recv()
        origin = lax.rem(me + (n - j if d == 0 else j), n)
        batch, low = grads_of[b]
        block = held.at[batch, origin, low]
        flying[b, d, j] = send(block, block, nexts[d])

    y_args = (n_y, y, partial, y_send, y_recv, y_next, {})
    forward(0)
    for b in (0, 3):
        for d in (0, 1):
            reduce_step(*y_args, b, d, 0)
    exact_in = share_stats(stat_b, jnp.broadcast_to(columns_to_row(squares), (4, tokens)), 1)

    stream_in.wait_recv()
    stream_core = send(x_other.at[mine], x_other.at[mine], to_core)
    stream_core.wait_recv()
    scale_other = row_to_columns(scale_other)
    inv_other = row_to_columns(inv_first_other)
    for at, size in lanes:
        piece = x_other[:, at:at + size].astype(F32) + scale_other * steer[:, at:at + size]
        normed[1, :, at:at + size] = (piece * inv_other * gain[:, at:at + size]).astype(BF16)
    forward(1)
    for b in (1, 2):
        for d in (0, 1):
            reduce_step(*y_args, b, d, 0)
    for j in range(1, n_y // 2):
        for b in range(4):
            for d in (0, 1):
                reduce_step(*y_args, b, d, j)
    x_in = []
    for b, there in enumerate((to_xl, to_dp, to_diag)):
        y_block[b] = reduce_end(*y_args, b).astype(BF16)
        x_in.append(send(y_block.at[b], x_recv.at[b], there))
    own_block = reduce_end(*y_args, 3)

    for copy in exact_in:
        copy.wait_recv()
    inv = lax.rsqrt(total_stats(stat_b, 0)[0:1] / model_width + 1e-05)
    ratio = inv / inv_first
    cols[1] = row_to_columns(inv)
    cols[2] = row_to_columns(ratio)
    ratio_mine[...] = jnp.broadcast_to(ratio, ratio_mine.shape)
    for copy in x_in:
        copy.wait_recv()
    ratio_in = send(ratio_mine, ratio_theirs, to_dp)

    fix = cols[2, pl.ds(pl.multiple_of(hi * ROWS, ROWS), ROWS)][:, 0:1]
    acts_same = (own_block + x_recv[0].astype(F32)) * fix
    acts_cross = (x_recv[1].astype(F32) + x_recv[2].astype(F32)) * fix
    gate = jnp.where(first, acts_same, acts_cross)
    up = jnp.where(first, acts_cross, acts_same)
    lane = lax.broadcasted_iota(jnp.int32, (ROWS, LANES), 1)
    low_gate = jnp.where(lane < RANK, gate[:, hidden:], 0.0).astype(BF16)
    low_up = jnp.where((lane >= RANK) & (lane < 2 * RANK), up[:, hidden:], 0.0).astype(BF16)
    factors = up_ext[:, 0:hidden]
    gate = gate[:, 0:hidden] + ADAPTER_SCALE * jnp.dot(low_gate, factors, preferred_element_type=F32)
    up = up[:, 0:hidden] + ADAPTER_SCALE * jnp.dot(low_up, factors, preferred_element_type=F32)
    sigma = 1.0 / (1.0 + jnp.exp(-gate))
    flow = cot_ref[...].astype(F32)
    gate_grad = (flow * up * sigma * (1.0 + gate * (1.0 - sigma))).astype(BF16)
    upper_grad = (flow * gate * sigma).astype(BF16)

    def ext_columns(low, grad, acts):
        inner = jnp.sum(grad.astype(F32) * acts, axis=1, keepdims=True)
        high = inner.astype(BF16).astype(F32)
        rest = jnp.where(lane == 32, high, jnp.where(lane == 33, inner - high, 0.0))
        return low.astype(F32) + rest

    gate_ext = ext_columns(low_gate, gate_grad, gate)
    upper_ext = ext_columns(low_up, upper_grad, up)
    gate_grad, upper_grad = gate_grad.astype(F32), upper_grad.astype(F32)
    acts_all[0, y, xl, :, 0:hidden] = jnp.where(first, gate_grad, upper_grad).astype(BF16)
    acts_all[0, y, xl, :, hidden:] = jnp.where(first, gate_ext, upper_ext).astype(BF16)
    acts_other[:, 0:hidden] = jnp.where(first, upper_grad, gate_grad).astype(BF16)
    acts_other[:, hidden:] = jnp.where(first, upper_ext, gate_ext).astype(BF16)

    x_out = [
        send(acts_all.at[0, y, xl], acts_all.at[0, y, xl], to_xl),
        send(acts_other, acts_all.at[1, y, xl], to_dp),
        send(acts_other, acts_all.at[1, y, xl], to_diag),
    ]
    g_args = (n_y, y, acts_all, y_next, {})
    for b in range(4):
        if b:
            x_out[b - 1].wait_recv()
        for d in (0, 1):
            gather_step(*g_args, b, d, 0)

    lane64 = lax.broadcasted_iota(jnp.int32, (4 * ROWS, LANES), 1)
    keep = ((lane64 >= RANK * dp) & (lane64 < RANK * dp + RANK)) | (lane64 == 32)
    half_z = n_z // 2

    def backward(slots, origins):
        shape = (2, 2, ROWS)
        rows = [acts_all[s, o].reshape(2 * ROWS, hidden + LANES) for o in origins for s in (0, 1)]
        rows = jnp.concatenate(rows, axis=0)
        for at, size in tiles(width, 256):
            block = lax.dot_general(
                rows[:, 0:hidden], w_buf[at:at + size, :], NT, preferred_element_type=F32
            )
            for i, q in enumerate(slots):
                back[q, :, :, :, at:at + size] = block[i * 64:(i + 1) * 64].reshape(*shape, size)
        block = lax.dot_general(rows, up_ext[...], NT, preferred_element_type=F32)
        for i, q in enumerate(slots):
            piece = jnp.where(keep, block[i * 64:(i + 1) * 64], 0.0)
            back[q, :, :, :, width:] = piece.reshape(*shape, LANES)
        return [send(back.at[q, :, 1 - core], core_recv.at[q], to_core) for q in slots]

    def scatter(slots, origins, core_in):
        for q, origin, copy in zip(slots, origins, core_in):
            copy.wait_recv()
            value = back[q, :, core] + core_recv[q]
            z_send[q] = value.astype(BF16)
            owner = lax.rem(origin + half_z * core, n_z)
            there = pltpu.make_async_remote_copy(
                src_ref=z_send.at[q, 1], dst_ref=z_recv.at[1, z],
                send_sem=z_send_sem.at[1, q], recv_sem=z_recv_sem.at[1, z],
                device_id={"dp": 1 - dp, "ffn": owner * 2 + core}, device_id_type=MESH,
            )
            here = pltpu.make_async_remote_copy(
                src_ref=z_send.at[q, 0], dst_ref=z_recv.at[0, z],
                send_sem=z_send_sem.at[0, q], recv_sem=z_recv_sem.at[0, z],
                device_id={"ffn": owner * 2 + core}, device_id_type=MESH,
            )
            there.start()
            started.append(there)

            @pl.when(owner != z)
            def _():
                here.start()

            @pl.when(owner == z)
            def _():
                own_sum[...] = value[0]

            z_started.append((owner, here))

    z_started = []
    waiting = None
    for j in range(n_y // 2 + 1):
        if j == 0:
            slots, origins = [0], [y]
        elif j == n_y // 2:
            slots, origins = [n_y - 1], [lax.rem(y + j, n_y)]
        else:
            slots, origins = [2 * j - 1, 2 * j], [lax.rem(y + n_y - j, n_y), lax.rem(y + j, n_y)]
        if j:
            for b in range(4):
                for d in (0, 1):
                    if j < hops(n_y, b, d):
                        gather_step(*g_args, b, d, j)
                    elif j == hops(n_y, b, d):
                        g_args[-1][b, d, j - 1].wait_recv()
        core_in = backward(slots, origins)
        if waiting is not None:
            scatter(*waiting)
        waiting = (slots, origins, core_in)
    scatter(*waiting)

    total = jnp.zeros((RANK, hidden), F32)
    for s in (0, 1):
        low = acts_all[s, :, :, :, hidden:].reshape(tokens, LANES).astype(F32)
        low = jnp.transpose(low)
        low = jnp.where(first, low[0:RANK], low[RANK:2 * RANK]).astype(BF16)
        rows = acts_all[s, :, :, :, 0:hidden].reshape(tokens, hidden)
        total += jnp.dot(low, rows, preferred_element_type=F32)
    up_mine[...] = ADAPTER_SCALE * total
    up_in = send(up_mine, up_theirs, to_dp)

    def arrived(from_other, source):
        pltpu.make_async_remote_copy(
            src_ref=z_send.at[0, 0], dst_ref=z_recv.at[from_other, source],
            send_sem=z_send_sem.at[0, 0], recv_sem=z_recv_sem.at[from_other, source],
            device_id=to_dp, device_id_type=MESH,
        ).wait_recv()

    for i in range(1, n_z):
        arrived(0, lax.rem(z + i, n_z))
    for i in range(n_z):
        arrived(1, i)
    total = own_sum[...]
    for i in range(1, n_z):
        total = total + z_recv[0, lax.rem(z + i, n_z)].astype(F32)
    for i in range(n_z):
        total = total + z_recv[1, i].astype(F32)

    held = lax.rem(z + n_z - half_z * core, n_z)
    share = pl.ds(pl.multiple_of((held * 2 + core) * ROWS, ROWS), ROWS)
    own_ext = total[:, width:]
    low_own = own_ext.astype(BF16)
    normed_grad = total[:, 0:width] + ADAPTER_SCALE * jnp.dot(
        low_own, down_ext[...], preferred_element_type=F32
    )
    inv_here = cols[1, share]
    inner = jnp.sum(jnp.where(lane == 32, own_ext, 0.0), axis=1, keepdims=True) / model_width
    pull = inv_here * inv_here * inner
    for at, size in lanes:
        gathered[held, core, :, at:at + size] = (
            inv_here * gain[:, at:at + size] * normed_grad[:, at:at + size]
            - pull * steered[share, at:at + size]
        ).astype(BF16)
    gathered[held, core, :, width:] = low_own
    low_mine[...] = low_own

    def spread(source_z, i):
        block = lax.rem(source_z + n_z - half_z * core, n_z)
        target = lax.rem(z + i, n_z) * 2 + core
        return pltpu.make_async_remote_copy(
            src_ref=gathered.at[block, core], dst_ref=gathered.at[block, core],
            send_sem=g_send_sem.at[0, i], recv_sem=g_recv_sem.at[0, source_z],
            device_id={"ffn": target}, device_id_type=MESH,
        )

    def spread_low(source_z, i):
        block = lax.rem(source_z + n_z - half_z * core, n_z)
        target = lax.rem(z + i, n_z) * 2 + core
        return pltpu.make_async_remote_copy(
            src_ref=low_mine, dst_ref=low_theirs.at[core, block],
            send_sem=g_send_sem.at[1, i], recv_sem=g_recv_sem.at[1, source_z],
            device_id={"dp": 1 - dp, "ffn": target}, device_id_type=MESH,
        )

    order = [0] + [i for j in range(1, half_z + 1) for i in dict.fromkeys((j, n_z - j))]
    for i in order[1:]:
        copy = spread(z, i)
        copy.start()
        started.append(copy)
    for i in order:
        copy = spread_low(z, i)
        copy.start()
        started.append(copy)
    from_core = []
    for i in order:
        source = lax.rem(z + n_z - i, n_z)
        block = lax.rem(source + n_z - half_z * core, n_z)
        if i:
            spread(source, i).wait_recv()
        from_core.append(send(gathered.at[block, core], gathered.at[block, core], to_core))
    for i in order:
        spread_low(lax.rem(z + n_z - i, n_z), i).wait_recv()
    from_core.append(send(low_theirs.at[core], low_theirs.at[core], to_core))
    for copy in from_core:
        copy.wait_recv()

    for at, size in lanes:
        piece = gathered[:, :, :, at:at + size].reshape(tokens, size)
        out_ref[:, at:at + size] = piece
        steer_mine[:, at:at + size] = jnp.sum(cols[0] * piece.astype(F32), axis=0, keepdims=True)
    steer_in = send(steer_mine, steer_theirs, to_dp)
    lows = (
        gathered[:, :, :, width:].reshape(tokens, LANES),
        jnp.concatenate([low_theirs[c, o] for o in range(n_z) for c in (0, 1)], axis=0),
    )
    down = []
    ratio_in.wait_recv()
    ratios = (ratio, ratio_theirs[0:1])
    for s in (0, 1):
        low = jnp.transpose(lows[s].astype(F32))[0:2 * RANK] * ratios[s]
        down.append(jnp.dot(low.astype(BF16), normed[s], preferred_element_type=F32))
    down_grad_ref[...] = ADAPTER_SCALE * (down[0] + down[1])
    up_in.wait_recv()
    up_grad_ref[dp] = up_mine[...]
    up_grad_ref[1 - dp] = up_theirs[...]
    steer_in.wait_recv()
    steer_grad_ref[...] = steer_mine[...] + steer_theirs[...]
    for copy in started:
        copy.wait_send()
    for owner, copy in z_started:

        @pl.when(owner != z)
        def _(copy=copy):
            copy.wait_send()


def hand_over(*refs):
    n = len(refs) // 2
    for i in range(n):
        refs[n + i][...] = refs[i][...]


def solution(mesh):
    n_hid, n_ffn = mesh.shape["hid"], mesh.shape["ffn"]
    n_y, n_z = n_hid // 2, n_ffn // 2

    def local(stream, steering, strength, gain, weights, down, up, cotangent):
        tokens, width = stream.shape
        hidden = weights.shape[2]
        vmem = pl.BlockSpec(memory_space=pltpu.VMEM)
        ext = hidden + LANES
        y_hop = (4, 2, n_y // 2, ROWS, ext)
        scratch = [
            ((width, hidden), BF16),
            ((tokens, width), BF16),
            ((2, n_hid, 4, tokens), F32),
            ((1, n_hid, 4, tokens), F32),
            ((4, tokens), F32),
            ((4, tokens), F32),
            ((tokens, width), F32),
            ((3, tokens, LANES), F32),
            ((2, tokens, width), BF16),
            ((2, n_y, 2, ROWS, ext), F32),
            (y_hop, BF16),
            (y_hop, BF16),
            ((3, ROWS, ext), BF16),
            ((3, ROWS, ext), BF16),
            ((LANES, ext), BF16),
            ((LANES, width), BF16),
            ((2, n_y, 2, ROWS, ext), BF16),
            ((ROWS, ext), BF16),
            ((n_z, 2, 2, ROWS, width + LANES), F32),
            ((n_z, 2, ROWS, width + LANES), F32),
            ((n_z, 2, ROWS, width + LANES), BF16),
            ((2, n_z, ROWS, width + LANES), BF16),
            ((ROWS, width + LANES), F32),
            ((n_z, 2, ROWS, width + LANES), BF16),
            ((ROWS, LANES), BF16),
            ((2, n_z, ROWS, LANES), BF16),
            ((RANK, hidden), F32),
            ((RANK, hidden), F32),
            ((1, width), F32),
            ((1, width), F32),
        ]
        model_width = width * n_hid
        residual, steer_grad, down_grad, up_grad = pl.pallas_call(
            functools.partial(kernel, model_width, n_hid, n_ffn),
            out_shape=(
                jax.ShapeDtypeStruct((tokens, width), BF16),
                jax.ShapeDtypeStruct((1, width), F32),
                jax.ShapeDtypeStruct((2 * RANK, width), F32),
                jax.ShapeDtypeStruct((2, RANK, hidden), F32),
            ),
            in_specs=[vmem] * 4 + [pl.BlockSpec(memory_space=pl.ANY)] + [vmem] * 3,
            out_specs=(vmem,) * 4,
            scratch_shapes=[pltpu.VMEM(shape, dtype) for shape, dtype in scratch]
            + [
                pltpu.SemaphoreType.DMA((N_SEMS,)),
                pltpu.SemaphoreType.DMA((N_SEMS,)),
                pltpu.SemaphoreType.DMA((2, n_z)),
                pltpu.SemaphoreType.DMA((2, n_z)),
                pltpu.SemaphoreType.DMA((2, n_z)),
                pltpu.SemaphoreType.DMA((2, n_z)),
                pltpu.SemaphoreType.DMA,
            ],
            compiler_params=pltpu.CompilerParams(
                collective_id=0, has_side_effects=True, vmem_limit_bytes=60 * 1024 * 1024
            ),
            cost_estimate=pl.CostEstimate(
                flops=8 * tokens * width * hidden, bytes_accessed=2 * width * hidden, transcendentals=0
            ),
        )(
            stream,
            steering.reshape(1, width),
            strength.reshape(1, tokens),
            gain.reshape(1, width),
            weights.reshape(width, hidden),
            jnp.transpose(down, (0, 2, 1)).reshape(2 * RANK, width),
            up.reshape(2 * RANK, hidden),
            cotangent,
        )
        results = (residual, steer_grad, down_grad, up_grad)
        residual, steer_grad, down_grad, up_grad = pl.pallas_call(
            hand_over,
            out_shape=tuple(jax.ShapeDtypeStruct(r.shape, r.dtype) for r in results),
            in_specs=[vmem] * 4,
            out_specs=(vmem,) * 4,
        )(*results)
        return (
            residual,
            steer_grad.reshape(width),
            jnp.transpose(down_grad.reshape(2, RANK, width), (0, 2, 1)),
            up_grad,
        )

    in_specs = (
        P("dp", "hid"),
        P("hid"),
        P("dp"),
        P("hid"),
        P("dp", "hid", "ffn"),
        P(None, "hid", None),
        P(None, None, "ffn"),
        P(("dp", "hid"), "ffn"),
    )
    out_specs = (P("dp", "hid"), P("hid"), P(None, "hid", None), P(None, None, "ffn"))
    return jax.shard_map(local, mesh=mesh, in_specs=in_specs, out_specs=out_specs, check_vma=False)
```
